32 devices in a mesh: parts: 2 (over y), row: 8 (over z, x), col: 2 (over core).
Axes of the slice: x: 2, y: 2, z: 4, core: 2. Of those that a mesh axis runs over, the one named last changes fastest.
Arguments:
- amplitudes: bfloat16 [16, 2, 2048, 256], P(('parts', 'row'), 'col'), parts along dimension 0, may hold values from -6 to 6
- integrals: bfloat16 [4, 2048, 2, 256], P(('parts', 'col')), parts along dimension 0, may hold values from -0.25 to 0.25
- orbital_irrep: int32 [16], P('parts'), parts along dimension 0, may hold values from 0 to 7, as said below
- slab_irrep: int32 [8], P('parts'), parts along dimension 0, may hold values from 0 to 7
- virtual_count: int32 [16], P('parts'), parts along dimension 0, may hold values from 128 to 256, as said below
Outputs:
- residual: bfloat16 [16, 2, 2048, 256], P('parts', 'col', 'row'), parts along dimension 0
The draws below stay inside these ranges and needn't reach their ends.
There are 2 independent parts, one for each index of `parts`. The reference program is written for one: setup_inputs(seed, part) draws one part's arguments, and reference() takes and returns one part's arrays. A program takes and returns all parts, laid end to end along the dimension named above; each array names one. Nothing has to cross between parts.
Inputs may be any that keep to these rules, and one draw needn't show every extreme that they name: orbital_irrep never falls along the orbitals i; each irrep labels at most 2 of them, and some irrep exactly 2. `virtual_count`: some irrep has all 256 places real.
All inputs are finite; a program needn't handle non-finite values.
Results may differ from the reference program's by a relative error of at most 0.001.
Values may be sent and summed in bfloat16 or wider, within the bound.
A program may use at most 64 MiB of HBM per device.

```python
import jax
import jax.numpy as jnp
from jax import lax

NIRR = 8
VI = 256
V = 2048
I = 8
IMAX = 2
K = 2
J = 2


def draw_orbital_irrep(key, part):
    key = jax.random.fold_in(key, 11)
    pick_key, slot_key = jax.random.split(key)
    full_irrep = jax.random.randint(pick_key, (), 0, NIRR)
    slot_order = jax.random.permutation(slot_key, (NIRR - 1) * IMAX)
    chosen_slots = slot_order[:I - IMAX]
    other_bins = chosen_slots // IMAX
    symmetries = jnp.arange(NIRR, dtype=jnp.int32)
    others = jnp.arange(NIRR - 1, dtype=jnp.int32)
    other_counts = jnp.sum((other_bins[:, None] == others[None, :]).astype(jnp.int32), axis=0)
    mapped = others + (others >= full_irrep).astype(jnp.int32)
    counts = jnp.sum(jnp.where(mapped[:, None] == symmetries[None, :], other_counts[:, None], 0), axis=0)
    counts = counts + jnp.where(symmetries == full_irrep, IMAX, 0)
    bounds = jnp.cumsum(counts)
    positions = jnp.arange(I, dtype=jnp.int32)
    return jnp.sum((positions[:, None] >= bounds[None, :]).astype(jnp.int32), axis=1).astype(jnp.int32)


def draw_virtual_count(key, part):
    key = jax.random.fold_in(key, 23)
    pick_key, size_key = jax.random.split(key)
    full_irrep = jax.random.randint(pick_key, (), 0, NIRR)
    drawn_sizes = jax.random.randint(size_key, (NIRR,), VI // 2, VI + 1)
    return jnp.where(jnp.arange(NIRR) == full_irrep, VI, drawn_sizes).astype(jnp.int32)


def touch_ends(result, key, smallest, high):
    extent = result.shape
    spot = [jax.random.randint(jax.random.fold_in(key, axis), (), 0, extent[axis]) for axis in range(len(extent))]
    result = result.at[tuple(spot)].set(smallest)
    longest = extent.index(max(extent))
    spot[longest] = (spot[longest] + 1) % extent[longest]
    return result.at[tuple(spot)].set(high)


def level_of(rng, shape, cuts, smallest, high):
    factor_of, own = 1.0, jax.random.fold_in(rng, 6)
    for dim, shards_of in cuts:
        draws = jnp.exp(jax.random.uniform(jax.random.fold_in(own, dim), (shards_of,), jnp.float32, smallest / len(cuts), high / len(cuts)))
        factor_of = factor_of * jnp.repeat(draws, shape[dim] // shards_of).reshape([-1 if axis == dim else 1 for axis in range(len(shape))])
    return factor_of


def bell_draw(key, shape, scale, limit, cuts=(), kind=jnp.bfloat16):
    result = scale * jax.random.normal(key, shape, jnp.float32)
    if cuts:
        result = result * level_of(key, shape, cuts, -0.22, 0.18)
    return jnp.clip(result, -limit, limit).astype(kind)


def setup_inputs(seed: int = 0, part: int = 0) -> dict:
    key_list = jax.random.split(jax.random.key(seed), 6)
    part_splits = jax.random.split(jax.random.fold_in(key_list[5], part), 6)
    return {
        "amplitudes": bell_draw(part_splits[0], (I, K, V, VI), 1.0, 6.0, ((0, 8), (1, 2))),
        "integrals": bell_draw(part_splits[1], (K, V, J, VI), (K * VI) ** -0.5, 0.25, ((0, 2),)),
        "orbital_irrep": draw_orbital_irrep(jax.random.fold_in(jax.random.fold_in(key_list[5], part), 71), part),
        "slab_irrep": touch_ends(jax.random.randint(part_splits[3], (K + J,), 0, NIRR), jax.random.fold_in(part_splits[3], 1), 0, NIRR - 1).astype(jnp.int32),
        "virtual_count": draw_virtual_count(jax.random.fold_in(jax.random.fold_in(key_list[5], part), 71), part),
    }


def lookup_count(virtual_count, symmetry):
    symmetries = jnp.arange(NIRR, dtype=jnp.int32)
    return jnp.sum(jnp.where(symmetry[..., None] == symmetries, virtual_count, 0), axis=-1)


def reference(amplitudes, integrals, orbital_irrep, slab_irrep, virtual_count):
    symmetries = jnp.arange(NIRR, dtype=jnp.int32)
    places = jnp.arange(VI, dtype=jnp.int32)
    pair_labels = slab_irrep[:K]
    column_labels = slab_irrep[K:]
    integral_tiles = integrals.reshape(K, NIRR, VI, J, VI)
    inner_keep = places[None, :] < virtual_count[:, None]
    outer_block = symmetries[None, :, None] ^ pair_labels[:, None, None] ^ column_labels[None, None, :]
    outer_keep = places < lookup_count(virtual_count, outer_block)[..., None]
    keep_mask = inner_keep[None, :, :, None, None] & outer_keep[:, :, None, :, :]
    kept_tiles = jnp.where(keep_mask, integral_tiles, jnp.zeros((), integrals.dtype))
    row_keep = inner_keep.reshape(NIRR * VI)
    slab_index = jnp.arange(K, dtype=jnp.int32)

    def one_orbital(operands):
        orbital_rows, own_label = operands
        block_index = symmetries[:, None] ^ own_label ^ pair_labels[None, :]
        selected = kept_tiles[slab_index[None, :], block_index].astype(jnp.float32)
        amplitude_grid = orbital_rows.reshape(K, NIRR, VI, VI).astype(jnp.float32)
        cycle_term = jnp.einsum("kgac,gkcjb->jgab", amplitude_grid, selected, precision=lax.Precision.HIGHEST)
        cycle_term = cycle_term.reshape(J, NIRR * VI, VI)
        return jnp.where(row_keep[None, :, None], cycle_term, 0.0).astype(jnp.bfloat16)

    return lax.map(one_orbital, (amplitudes, orbital_irrep))
```

```python
import functools

import jax
import jax.numpy as jnp
from jax import lax
from jax.experimental import pallas as pl
from jax.experimental.pallas import tpu as pltpu
from jax.sharding import PartitionSpec as P

MESH = pl.DeviceIdType.MESH


def partner_of(me, step, count):
    if count & (count - 1):
        return (me + step) % count
    place, bit = 0, 1
    while bit < count:
        place = place + (((me // bit) % 2 + (step // bit) % 2) % 2) * bit
        bit *= 2
    return place


def each(low, high, body):
    if high - low <= 16:
        for step in range(low, high):
            body(step)
    else:
        lax.fori_loop(low, high, lambda step, carry: (body(step), carry)[1], 0)


def kernel(
    count,
    label_ref, slab_ref, size_ref, amp_ref, int_ref, out_ref,
    landed, shared, staged, raw, own_tiles, sent_tiles, other_tiles,
    send_sem, land_sem, pass_sem, share_sem, out_sem, raw_sem, tile_sem, own_sem,
):
    me = lax.axis_index("row")
    col = lax.axis_index("col")
    sibling = 1 - col
    rows = landed.shape[1]
    width = landed.shape[2]
    groups = own_tiles.shape[0]

    raw_copies = [
        pltpu.make_async_copy(
            int_ref.at[0, pl.ds(e * width, width)], raw.at[e], raw_sem.at[e]
        )
        for e in range(groups)
    ]
    own_copy = pltpu.make_async_copy(
        amp_ref.at[0, 0, pl.ds(pl.multiple_of(me * rows, rows), rows)], landed.at[me], own_sem
    )

    barrier = pltpu.get_barrier_semaphore()

    def greet(step):
        pl.semaphore_signal(
            barrier, inc=1, device_id={"row": partner_of(me, step, count)}, device_id_type=MESH
        )

    each(1, count, greet)
    pl.semaphore_signal(barrier, inc=1, device_id={"col": sibling}, device_id_type=MESH)
    pl.semaphore_wait(barrier, count)

    def spread_copy(step):
        there = partner_of(me, step, count)
        return pltpu.make_async_remote_copy(
            src_ref=amp_ref.at[0, 0, pl.ds(pl.multiple_of(there * rows, rows), rows)],
            dst_ref=landed.at[me],
            send_sem=send_sem.at[step],
            recv_sem=land_sem.at[step],
            device_id={"row": there},
            device_id_type=MESH,
        )

    each(1, count, lambda step: spread_copy(count - step).start())
    own_copy.start()
    for copy in raw_copies:
        copy.start()

    own_label = slab_ref[col]
    place = lax.broadcasted_iota(jnp.int32, (width, width), 0)
    column = lax.broadcasted_iota(jnp.int32, (width, width), 1)

    def keep(tile, e, j):
        outer = size_ref[e ^ own_label ^ slab_ref[2 + j]]
        return jnp.where((place < size_ref[e]) & (column < outer), tile, jnp.zeros((), tile.dtype))

    tile_copies = []
    for e in range(groups):
        raw_copies[e].wait()
        tile_pair = raw[e]
        first = tile_pair[:, 0, :]
        second = tile_pair[:, 1, :]
        mine = jnp.where(col == 0, first, second)
        other = jnp.where(col == 0, second, first)
        sent_tiles[e] = keep(other, e, sibling)
        copy = pltpu.make_async_remote_copy(
            src_ref=sent_tiles.at[e],
            dst_ref=other_tiles.at[e],
            send_sem=tile_sem.at[0, e],
            recv_sem=tile_sem.at[1, e],
            device_id={"col": sibling},
            device_id_type=MESH,
        )
        copy.start()
        tile_copies.append(copy)
        own_tiles[e] = keep(mine, e, col)

    def share_copy(step):
        source = partner_of(me, step, count)
        return pltpu.make_async_remote_copy(
            src_ref=landed.at[source],
            dst_ref=shared.at[source],
            send_sem=pass_sem.at[step],
            recv_sem=share_sem.at[step],
            device_id={"col": sibling},
            device_id_type=MESH,
        )

    first_virtual = me * rows
    group = first_virtual // width
    offset = first_virtual % width
    row_place = lax.broadcasted_iota(jnp.int32, (rows, width), 0) + offset
    row_keep = row_place < size_ref[group]
    other_label = slab_ref[sibling]

    def out_copy(step):
        source = partner_of(me, step, count)
        return pltpu.make_async_copy(staged.at[source], out_ref.at[source, 0], out_sem.at[step])

    def finish(step):
        source = partner_of(me, step, count)
        share_copy(step).wait_recv()
        label = group ^ label_ref[source]
        total = jnp.dot(
            landed[source], own_tiles[label ^ own_label], preferred_element_type=jnp.float32
        )
        total = total + jnp.dot(
            shared[source], other_tiles[label ^ other_label], preferred_element_type=jnp.float32
        )
        staged[source] = jnp.where(row_keep, total, 0.0).astype(staged.dtype)
        out_copy(step).start()

    own_copy.wait()
    share_copy(0).start()
    for copy in tile_copies:
        copy.wait_recv()

    def arrive(step):
        spread_copy(step).wait_recv()
        share_copy(step).start()
        finish(step - 1)

    each(1, count, arrive)
    finish(count - 1)

    for copy in tile_copies:
        copy.wait_send()
    each(1, count, lambda step: spread_copy(step).wait_send())
    each(0, count, lambda step: share_copy(step).wait_send())
    each(0, count, lambda step: out_copy(step).wait())


def per_device(amplitudes, integrals, orbital_irrep, slab_irrep, virtual_count, count):
    virtual_total, width = amplitudes.shape[2:]
    groups = virtual_count.shape[0]
    rows = virtual_total // count
    kind = amplitudes.dtype
    smem = pl.BlockSpec(memory_space=pltpu.SMEM)
    anywhere = pl.BlockSpec(memory_space=pl.ANY)
    dma = pltpu.SemaphoreType.DMA
    return pl.pallas_call(
        functools.partial(kernel, count),
        out_shape=jax.ShapeDtypeStruct((count, 1, rows, width), kind),
        in_specs=[smem, smem, smem, anywhere, anywhere],
        out_specs=anywhere,
        scratch_shapes=[
            pltpu.VMEM((count, rows, width), kind),
            pltpu.VMEM((count, rows, width), kind),
            pltpu.VMEM((count, rows, width), kind),
            pltpu.VMEM((groups, width, 2, width), kind),
            pltpu.VMEM((groups, width, width), kind),
            pltpu.VMEM((groups, width, width), kind),
            pltpu.VMEM((groups, width, width), kind),
            dma((count,)),
            dma((count,)),
            dma((count,)),
            dma((count,)),
            dma((count,)),
            dma((groups,)),
            dma((2, groups)),
            dma,
        ],
        compiler_params=pltpu.CompilerParams(
            collective_id=0, has_side_effects=True, vmem_limit_bytes=48 * 1024 * 1024
        ),
    )(orbital_irrep, slab_irrep, virtual_count, amplitudes, integrals)


def solution(mesh):
    in_specs = (
        P(("parts", "row"), "col", None, None),
        P(("parts", "col"), None, None, None),
        P("parts"),
        P("parts"),
        P("parts"),
    )
    return jax.shard_map(
        functools.partial(per_device, count=mesh.shape["row"]),
        mesh=mesh,
        in_specs=in_specs,
        out_specs=P("parts", "col", "row", None),
        check_vma=False,
    )
```

```python
import functools

import jax
import jax.numpy as jnp
from jax import lax
from jax.experimental import pallas as pl
from jax.experimental.pallas import tpu as pltpu
from jax.sharding import PartitionSpec as P

MESH = pl.DeviceIdType.MESH


def partner_of(me, step, count, back=False):
    if count & (count - 1):
        return (me + (count - step if back else step)) % count
    place, bit = 0, 1
    while bit < count:
        place = place + (((me // bit) % 2 + (step // bit) % 2) % 2) * bit
        bit *= 2
    return place


def each(low, high, body):
    if high - low <= 16:
        for step in range(low, high):
            body(step)
    else:
        lax.fori_loop(low, high, lambda step, carry: (body(step), carry)[1], 0)


def kernel(
    count,
    label_hbm, slab_hbm, size_hbm, amp_ref, int_ref, out_ref,
    label_ref, slab_ref, size_ref, landed, shared, staged, raw, own_tiles, sent_tiles, other_tiles,
    send_sem, land_sem, pass_sem, share_sem, out_sem, raw_sem, tile_sem, own_sem, label_sem,
):
    me = lax.axis_index("row")
    col = lax.axis_index("col")
    sibling = 1 - col
    rows = landed.shape[1]
    width = landed.shape[2]
    groups = own_tiles.shape[0]

    raw_copies = [
        pltpu.make_async_copy(
            int_ref.at[0, pl.ds(e * width, width)], raw.at[e], raw_sem.at[e]
        )
        for e in range(groups)
    ]
    own_copy = pltpu.make_async_copy(
        amp_ref.at[0, 0, pl.ds(pl.multiple_of(me * rows, rows), rows)], landed.at[me], own_sem
    )

    label_copies = [
        pltpu.make_async_copy(source, place, label_sem.at[number])
        for number, (source, place) in enumerate(
            [(label_hbm, label_ref), (slab_hbm, slab_ref), (size_hbm, size_ref)]
        )
    ]
    for copy in label_copies + raw_copies:
        copy.start()
    own_copy.start()

    barrier = pltpu.get_barrier_semaphore()

    def greet(step):
        pl.semaphore_signal(
            barrier, inc=1, device_id={"row": partner_of(me, step, count)}, device_id_type=MESH
        )

    each(1, count, greet)
    pl.semaphore_signal(barrier, inc=1, device_id={"col": sibling}, device_id_type=MESH)
    pl.semaphore_wait(barrier, count)

    def spread_copy(step):
        there = partner_of(me, step, count)
        return pltpu.make_async_remote_copy(
            src_ref=amp_ref.at[0, 0, pl.ds(pl.multiple_of(there * rows, rows), rows)],
            dst_ref=landed.at[me],
            send_sem=send_sem.at[step],
            recv_sem=land_sem.at[step],
            device_id={"row": there},
            device_id_type=MESH,
        )

    each(1, count, lambda step: spread_copy(step).start())
    for copy in label_copies:
        copy.wait()

    own_label = slab_ref[col]
    place = lax.broadcasted_iota(jnp.int32, (width, width), 0)
    column = lax.broadcasted_iota(jnp.int32, (width, width), 1)

    def keep(tile, e, j):
        outer = size_ref[e ^ own_label ^ slab_ref[2 + j]]
        return jnp.where((place < size_ref[e]) & (column < outer), tile, jnp.zeros((), tile.dtype))

    tile_copies = []
    for e in range(groups):
        raw_copies[e].wait()
        tile_pair = raw[e]
        first = tile_pair[:, 0, :]
        second = tile_pair[:, 1, :]
        mine = jnp.where(col == 0, first, second)
        other = jnp.where(col == 0, second, first)
        sent_tiles[e] = keep(other, e, sibling)
        copy = pltpu.make_async_remote_copy(
            src_ref=sent_tiles.at[e],
            dst_ref=other_tiles.at[e],
            send_sem=tile_sem.at[0, e],
            recv_sem=tile_sem.at[1, e],
            device_id={"col": sibling},
            device_id_type=MESH,
        )
        copy.start()
        tile_copies.append(copy)
        own_tiles[e] = keep(mine, e, col)

    def share_copy(step):
        source = partner_of(me, step, count, back=True)
        return pltpu.make_async_remote_copy(
            src_ref=landed.at[source],
            dst_ref=shared.at[source],
            send_sem=pass_sem.at[step],
            recv_sem=share_sem.at[step],
            device_id={"col": sibling},
            device_id_type=MESH,
        )

    first_virtual = me * rows
    group = first_virtual // width
    offset = first_virtual % width
    row_place = lax.broadcasted_iota(jnp.int32, (rows, width), 0) + offset
    row_keep = row_place < size_ref[group]
    other_label = slab_ref[sibling]

    def out_copy(step):
        source = partner_of(me, step, count, back=True)
        return pltpu.make_async_copy(staged.at[source], out_ref.at[source, 0], out_sem.at[step])

    def finish(step):
        source = partner_of(me, step, count, back=True)
        share_copy(step).wait_recv()
        label = group ^ label_ref[source]
        total = jnp.dot(
            landed[source], own_tiles[label ^ own_label], preferred_element_type=jnp.float32
        )
        total = total + jnp.dot(
            shared[source], other_tiles[label ^ other_label], preferred_element_type=jnp.float32
        )
        staged[source] = jnp.where(row_keep, total, 0.0).astype(staged.dtype)
        out_copy(step).start()

    own_copy.wait()
    share_copy(0).start()
    for copy in tile_copies:
        copy.wait_recv()

    def arrive(step):
        spread_copy(step).wait_recv()
        share_copy(step).start()
        finish(step - 1)

    each(1, count, arrive)
    finish(count - 1)

    for copy in tile_copies:
        copy.wait_send()
    each(1, count, lambda step: spread_copy(step).wait_send())
    each(0, count, lambda step: share_copy(step).wait_send())
    each(0, count, lambda step: out_copy(step).wait())


def per_device(amplitudes, integrals, orbital_irrep, slab_irrep, virtual_count, count):
    virtual_total, width = amplitudes.shape[2:]
    groups = virtual_count.shape[0]
    rows = virtual_total // count
    kind = amplitudes.dtype
    anywhere = pl.BlockSpec(memory_space=pl.ANY)
    dma = pltpu.SemaphoreType.DMA
    return pl.pallas_call(
        functools.partial(kernel, count),
        out_shape=jax.ShapeDtypeStruct((count, 1, rows, width), kind),
        in_specs=[anywhere] * 5,
        out_specs=anywhere,
        scratch_shapes=[
            pltpu.SMEM(orbital_irrep.shape, jnp.int32),
            pltpu.SMEM(slab_irrep.shape, jnp.int32),
            pltpu.SMEM(virtual_count.shape, jnp.int32),
            pltpu.VMEM((count, rows, width), kind),
            pltpu.VMEM((count, rows, width), kind),
            pltpu.VMEM((count, rows, width), kind),
            pltpu.VMEM((groups, width, 2, width), kind),
            pltpu.VMEM((groups, width, width), kind),
            pltpu.VMEM((groups, width, width), kind),
            pltpu.VMEM((groups, width, width), kind),
            dma((count,)),
            dma((count,)),
            dma((count,)),
            dma((count,)),
            dma((count,)),
            dma((groups,)),
            dma((2, groups)),
            dma,
            dma((3,)),
        ],
        compiler_params=pltpu.CompilerParams(
            collective_id=0, has_side_effects=True, vmem_limit_bytes=62 * 1024 * 1024
        ),
    )(orbital_irrep, slab_irrep, virtual_count, amplitudes, integrals)


def solution(mesh):
    in_specs = (
        P(("parts", "row"), "col", None, None),
        P(("parts", "col"), None, None, None),
        P("parts"),
        P("parts"),
        P("parts"),
    )
    return jax.shard_map(
        functools.partial(per_device, count=mesh.shape["row"]),
        mesh=mesh,
        in_specs=in_specs,
        out_specs=P("parts", "col", "row", None),
        check_vma=False,
    )
```

```python
import functools

import jax
import jax.numpy as jnp
from jax import lax
from jax.experimental import pallas as pl
from jax.experimental.pallas import tpu as pltpu
from jax.sharding import PartitionSpec as P

MESH = pl.DeviceIdType.MESH


def partner_of(me, step, count, back=False):
    if count & (count - 1):
        return (me + (count - step if back else step)) % count
    place, bit = 0, 1
    while bit < count:
        place = place + (((me // bit) % 2 + (step // bit) % 2) % 2) * bit
        bit *= 2
    return place


def each(low, high, body):
    if high - low <= 16:
        for step in range(low, high):
            body(step)
    else:
        lax.fori_loop(low, high, lambda step, carry: (body(step), carry)[1], 0)


def kernel(
    count,
    label_hbm, slab_hbm, size_hbm, amp_ref, int_ref, out_ref,
    label_ref, slab_ref, size_ref, landed, shared, staged, raw, own_tiles, sent_tiles, other_tiles,
    send_sem, land_sem, pass_sem, share_sem, done_sem, own_sem, raw_sem, tile_sem, label_sem,
):
    me = lax.axis_index("row")
    col = lax.axis_index("col")
    sibling = 1 - col
    rows, width = landed.shape[1:]
    groups = own_tiles.shape[0]
    near, late = count // 2, count - count // 4

    def target(step):
        return partner_of(me, step, count)

    def source(step):
        return partner_of(me, step, count, back=True)

    def block_of(there):
        return amp_ref.at[0, 0, pl.ds(pl.multiple_of(there * rows, rows), rows)]

    raw_copies = [
        pltpu.make_async_copy(
            int_ref.at[0, pl.ds(e * width, width)], raw.at[e], raw_sem.at[e]
        )
        for e in range(groups)
    ]
    label_copies = [
        pltpu.make_async_copy(origin, place, label_sem.at[number])
        for number, (origin, place) in enumerate(
            [(label_hbm, label_ref), (slab_hbm, slab_ref), (size_hbm, size_ref)]
        )
    ]

    def own_copy(step):
        slot = source(step)
        return pltpu.make_async_copy(block_of(target(step)), landed.at[slot], own_sem.at[step])

    def spread_copy(step):
        there = target(step)
        return pltpu.make_async_remote_copy(
            src_ref=block_of(there),
            dst_ref=landed.at[me],
            send_sem=send_sem.at[step],
            recv_sem=land_sem.at[step],
            device_id={"row": there},
            device_id_type=MESH,
        )

    def share_copy(step, local):
        slot = source(step)
        return pltpu.make_async_remote_copy(
            src_ref=block_of(target(step)) if local else landed.at[slot],
            dst_ref=shared.at[slot],
            send_sem=pass_sem.at[step],
            recv_sem=share_sem.at[step],
            device_id={"col": sibling},
            device_id_type=MESH,
        )

    def done_copy(step):
        return pltpu.make_async_remote_copy(
            src_ref=staged.at[step - late],
            dst_ref=out_ref.at[me, 0],
            send_sem=send_sem.at[step],
            recv_sem=done_sem.at[step - late],
            device_id={"row": target(step)},
            device_id_type=MESH,
        )

    for copy in label_copies + raw_copies:
        copy.start()
    each(late, count, lambda step: own_copy(step).start())
    own_copy(0).start()

    barrier = pltpu.get_barrier_semaphore()

    def greet(step):
        pl.semaphore_signal(
            barrier, inc=1, device_id={"row": target(step)}, device_id_type=MESH
        )

    each(1, count, greet)
    pl.semaphore_signal(barrier, inc=1, device_id={"col": sibling}, device_id_type=MESH)
    pl.semaphore_wait(barrier, count)

    each(near, late, lambda step: spread_copy(step).start())
    each(1, near, lambda step: spread_copy(step).start())
    each(late, count, lambda step: share_copy(step, True).start())
    share_copy(0, True).start()
    for copy in label_copies:
        copy.wait()

    own_label = slab_ref[col]
    other_label = slab_ref[sibling]
    place = lax.broadcasted_iota(jnp.int32, (width, width), 0)
    column = lax.broadcasted_iota(jnp.int32, (width, width), 1)

    def keep(tile, e, j):
        outer = size_ref[e ^ own_label ^ slab_ref[2 + j]]
        return jnp.where((place < size_ref[e]) & (column < outer), tile, jnp.zeros((), tile.dtype))

    tile_copies = []
    for e in range(groups):
        raw_copies[e].wait()
        tile_pair = raw[e]
        first = tile_pair[:, 0, :]
        second = tile_pair[:, 1, :]
        mine = jnp.where(col == 0, first, second)
        other = jnp.where(col == 0, second, first)
        sent_tiles[e] = keep(other, e, sibling)
        copy = pltpu.make_async_remote_copy(
            src_ref=sent_tiles.at[e],
            dst_ref=other_tiles.at[e],
            send_sem=tile_sem.at[0, e],
            recv_sem=tile_sem.at[1, e],
            device_id={"col": sibling},
            device_id_type=MESH,
        )
        copy.start()
        tile_copies.append(copy)
        own_tiles[e] = keep(mine, e, col)
    for copy in tile_copies:
        copy.wait_recv()

    row_place = lax.broadcasted_iota(jnp.int32, (rows, width), 0)

    def product(slot, there, orbital):
        first_virtual = there * rows
        group = first_virtual // width
        label = group ^ label_ref[orbital]
        total = jnp.dot(
            landed[slot], own_tiles[label ^ own_label], preferred_element_type=jnp.float32
        )
        total = total + jnp.dot(
            shared[slot], other_tiles[label ^ other_label], preferred_element_type=jnp.float32
        )
        real = row_place + first_virtual % width < size_ref[group]
        return jnp.where(real, total, 0.0).astype(out_ref.dtype)

    def depart(step):
        own_copy(step).wait()
        share_copy(step, True).wait_recv()
        staged[step - late] = product(source(step), target(step), me)
        done_copy(step).start()

    each(late, count, depart)

    def finish(step):
        share_copy(step, False).wait_recv()
        out_ref[source(step), 0] = product(source(step), me, source(step))

    own_copy(0).wait()
    finish(0)

    def arrive(step):
        spread_copy(step).wait_recv()
        share_copy(step, False).start()

    def arrive_then_finish(step):
        arrive(step)
        finish(step - 1)

    arrive(1)
    each(2, near, arrive_then_finish)
    each(near, late, arrive_then_finish)
    finish(late - 1)

    for copy in tile_copies:
        copy.wait_send()
    each(1, late, lambda step: spread_copy(step).wait_send())
    each(late, count, lambda step: done_copy(step).wait_send())
    each(1, late, lambda step: share_copy(step, False).wait_send())
    each(late, count, lambda step: share_copy(step, True).wait_send())
    share_copy(0, True).wait_send()
    each(late, count, lambda step: done_copy(step).wait_recv())


def per_device(amplitudes, integrals, orbital_irrep, slab_irrep, virtual_count, count):
    virtual_total, width = amplitudes.shape[2:]
    groups = virtual_count.shape[0]
    rows = virtual_total // count
    late_count = count // 4
    kind = amplitudes.dtype
    dma = pltpu.SemaphoreType.DMA
    return pl.pallas_call(
        functools.partial(kernel, count),
        out_shape=pltpu.VMEM((count, 1, rows, width), kind),
        in_specs=[pl.BlockSpec(memory_space=pltpu.HBM)] * 5,
        out_specs=pl.BlockSpec(memory_space=pltpu.VMEM),
        scratch_shapes=[
            pltpu.SMEM(orbital_irrep.shape, jnp.int32),
            pltpu.SMEM(slab_irrep.shape, jnp.int32),
            pltpu.SMEM(virtual_count.shape, jnp.int32),
            pltpu.VMEM((count, rows, width), kind),
            pltpu.VMEM((count, rows, width), kind),
            pltpu.VMEM((late_count, rows, width), kind),
            pltpu.VMEM((groups, width, 2, width), kind),
            pltpu.VMEM((groups, width, width), kind),
            pltpu.VMEM((groups, width, width), kind),
            pltpu.VMEM((groups, width, width), kind),
            dma((count,)),
            dma((count,)),
            dma((count,)),
            dma((count,)),
            dma((late_count,)),
            dma((count,)),
            dma((groups,)),
            dma((2, groups)),
            dma((3,)),
        ],
        compiler_params=pltpu.CompilerParams(
            collective_id=0, has_side_effects=True, vmem_limit_bytes=48 * 1024 * 1024
        ),
    )(
        *[
            pltpu.with_memory_space_constraint(operand, pltpu.HBM)
            for operand in (orbital_irrep, slab_irrep, virtual_count, amplitudes, integrals)
        ]
    )


def solution(mesh):
    in_specs = (
        P(("parts", "row"), "col", None, None),
        P(("parts", "col"), None, None, None),
        P("parts"),
        P("parts"),
        P("parts"),
    )
    return jax.shard_map(
        functools.partial(per_device, count=mesh.shape["row"]),
        mesh=mesh,
        in_specs=in_specs,
        out_specs=P("parts", "col", "row", None),
        check_vma=False,
    )
```

```python
import functools

import jax
import jax.numpy as jnp
from jax import lax
from jax.experimental import pallas as pl
from jax.experimental.pallas import tpu as pltpu
from jax.sharding import PartitionSpec as P

MESH = pl.DeviceIdType.MESH


def partner_of(me, step, count, back=False):
    if count & (count - 1):
        return (me + (count - step if back else step)) % count
    place, bit = 0, 1
    while bit < count:
        place = place + (((me // bit) % 2 + (step // bit) % 2) % 2) * bit
        bit *= 2
    return place


def each(low, high, body):
    if high - low <= 16:
        for step in range(low, high):
            body(step)
    else:
        lax.fori_loop(low, high, lambda step, carry: (body(step), carry)[1], 0)


def kernel(
    count,
    label_hbm, slab_hbm, size_hbm, amp_ref, int_ref, out_ref,
    label_ref, slab_ref, size_ref, landed, shared, late_own, late_shared, staged, raw, own_tiles, sent_tiles, other_tiles,
    send_sem, land_sem, pass_sem, share_sem, late_sem, done_sem, own_sem, raw_sem, tile_sem, label_sem, ready_sem,
):
    me = lax.axis_index("row")
    col = lax.axis_index("col")
    sibling = 1 - col
    rows, width = landed.shape[1:]
    groups = own_tiles.shape[0]
    quarter = count // 4
    near, late = count // 2, count - quarter
    last = me // late
    odd = (me // quarter) % 2

    def target(step):
        return partner_of(me, step, count)

    def source(step):
        return partner_of(me, step, count, back=True)

    def block_of(there):
        return amp_ref.at[0, 0, pl.ds(pl.multiple_of(there * rows, rows), rows)]

    raw_copies = [
        pltpu.make_async_copy(
            int_ref.at[0, pl.ds(e * width, width)], raw.at[e], raw_sem.at[e]
        )
        for e in range(groups)
    ]
    label_copies = [
        pltpu.make_async_copy(origin, place, label_sem.at[number])
        for number, (origin, place) in enumerate(
            [(label_hbm, label_ref), (slab_hbm, slab_ref), (size_hbm, size_ref)]
        )
    ]

    def late_step(slot):
        return late + slot - quarter * odd

    own_copy = pltpu.make_async_copy(block_of(me), landed.at[me], own_sem.at[quarter])

    def late_copy(slot):
        return pltpu.make_async_copy(
            block_of(target(late_step(slot))), late_own.at[slot], own_sem.at[slot]
        )

    def late_share(slot):
        return pltpu.make_async_remote_copy(
            src_ref=block_of(target(late_step(slot))),
            dst_ref=late_shared.at[slot],
            send_sem=late_sem.at[0, slot],
            recv_sem=late_sem.at[1, slot],
            device_id={"col": sibling},
            device_id_type=MESH,
        )

    def spread_copy(step):
        there = target(step)
        return pltpu.make_async_remote_copy(
            src_ref=block_of(there),
            dst_ref=landed.at[me],
            send_sem=send_sem.at[step],
            recv_sem=land_sem.at[step],
            device_id={"row": there},
            device_id_type=MESH,
        )

    def share_copy(step):
        slot = source(step)
        return pltpu.make_async_remote_copy(
            src_ref=landed.at[slot],
            dst_ref=shared.at[slot],
            send_sem=pass_sem.at[step],
            recv_sem=share_sem.at[step],
            device_id={"col": sibling},
            device_id_type=MESH,
        )

    def done_copy(step, slot):
        return pltpu.make_async_remote_copy(
            src_ref=staged.at[slot],
            dst_ref=out_ref.at[me, 0],
            send_sem=send_sem.at[step],
            recv_sem=done_sem.at[step - near],
            device_id={"row": target(step)},
            device_id_type=MESH,
        )

    for copy in label_copies + raw_copies:
        copy.start()
    each(0, quarter, lambda slot: late_copy(slot).start())
    own_copy.start()

    barrier = pltpu.get_barrier_semaphore()

    def signal(semaphore, step):
        pl.semaphore_signal(
            semaphore, inc=1, device_id={"row": target(step)}, device_id_type=MESH
        )

    each(1, quarter, lambda step: signal(barrier, step))
    pl.semaphore_signal(barrier, inc=1, device_id={"col": sibling}, device_id_type=MESH)

    @pl.when(last == 0)
    def _():
        each(quarter, count, lambda step: signal(barrier, step))

    pl.semaphore_wait(barrier, count - quarter * (1 - last))

    @pl.when(last == 1)
    def _():
        each(quarter, count, lambda step: signal(ready_sem, step))

    def send_now(step):
        @pl.when(last + 1 > target(step) // late)
        def _():
            spread_copy(step).start()

    def send_when_ready(step):
        @pl.when(last < target(step) // late)
        def _():
            spread_copy(step).start()

    each(near, late, lambda step: spread_copy(step + quarter * odd).start())
    each(1, near, send_now)

    @pl.when(last == 0)
    def _():
        pl.semaphore_wait(ready_sem, quarter)

    each(1, near, send_when_ready)
    each(0, quarter, lambda slot: late_share(slot).start())
    for copy in label_copies:
        copy.wait()

    own_label = slab_ref[col]
    other_label = slab_ref[sibling]
    place = lax.broadcasted_iota(jnp.int32, (width, width), 0)
    column = lax.broadcasted_iota(jnp.int32, (width, width), 1)

    def keep(tile, e, j):
        outer = size_ref[e ^ own_label ^ slab_ref[2 + j]]
        return jnp.where((place < size_ref[e]) & (column < outer), tile, jnp.zeros((), tile.dtype))

    tile_copies = []
    for e in range(groups):
        raw_copies[e].wait()
        tile_pair = raw[e]
        first = tile_pair[:, 0, :]
        second = tile_pair[:, 1, :]
        mine = jnp.where(col == 0, first, second)
        other = jnp.where(col == 0, second, first)
        sent_tiles[e] = keep(other, e, sibling)
        copy = pltpu.make_async_remote_copy(
            src_ref=sent_tiles.at[e],
            dst_ref=other_tiles.at[e],
            send_sem=tile_sem.at[0, e],
            recv_sem=tile_sem.at[1, e],
            device_id={"col": sibling},
            device_id_type=MESH,
        )
        copy.start()
        tile_copies.append(copy)
        own_tiles[e] = keep(mine, e, col)
    for copy in tile_copies:
        copy.wait_recv()

    row_place = lax.broadcasted_iota(jnp.int32, (rows, width), 0)

    def product(mine, other, there, orbital):
        first_virtual = there * rows
        group = first_virtual // width
        label = group ^ label_ref[orbital]
        total = jnp.dot(
            mine, own_tiles[label ^ own_label], preferred_element_type=jnp.float32
        )
        total = total + jnp.dot(
            other, other_tiles[label ^ other_label], preferred_element_type=jnp.float32
        )
        real = row_place + first_virtual % width < size_ref[group]
        return jnp.where(real, total, 0.0).astype(out_ref.dtype)

    def depart(slot):
        late_copy(slot).wait()
        late_share(slot).wait_recv()
        step = late_step(slot)
        staged[slot] = product(late_own[slot], late_shared[slot], target(step), me)
        done_copy(step, slot).start()

    each(0, quarter, depart)

    own_copy.wait()
    share_copy(0).start()

    def finish(step):
        share_copy(step).wait_recv()
        there = source(step)
        out_ref[there, 0] = product(landed[there], shared[there], me, there)

    def arrive(step):
        spread_copy(step).wait_recv()
        share_copy(step).start()

    def arrive_then_finish(step):
        arrive(step)
        finish(step - 1)

    each(1, near, arrive_then_finish)

    @pl.when(odd == 0)
    def _():
        each(near, count, arrive_then_finish)
        finish(count - 1)

    @pl.when(odd == 1)
    def _():
        finish(near - 1)

    for copy in tile_copies:
        copy.wait_send()
    each(1, near, lambda step: spread_copy(step).wait_send())
    each(near, late, lambda step: spread_copy(step + quarter * odd).wait_send())
    each(0, quarter, lambda slot: done_copy(late_step(slot), slot).wait_send())
    each(0, quarter, lambda slot: late_share(slot).wait_send())
    each(0, near, lambda step: share_copy(step).wait_send())

    @pl.when(odd == 0)
    def _():
        each(near, count, lambda step: share_copy(step).wait_send())

    @pl.when(odd == 1)
    def _():
        each(near, count, lambda step: done_copy(step, 0).wait_recv())


def per_device(amplitudes, integrals, orbital_irrep, slab_irrep, virtual_count, count):
    virtual_total, width = amplitudes.shape[2:]
    groups = virtual_count.shape[0]
    rows = virtual_total // count
    quarter = count // 4
    kind = amplitudes.dtype
    dma = pltpu.SemaphoreType.DMA
    return pl.pallas_call(
        functools.partial(kernel, count),
        out_shape=pltpu.VMEM((count, 1, rows, width), kind),
        in_specs=[pl.BlockSpec(memory_space=pltpu.HBM)] * 5,
        out_specs=pl.BlockSpec(memory_space=pltpu.VMEM),
        scratch_shapes=[
            pltpu.SMEM(orbital_irrep.shape, jnp.int32),
            pltpu.SMEM(slab_irrep.shape, jnp.int32),
            pltpu.SMEM(virtual_count.shape, jnp.int32),
            pltpu.VMEM((count, rows, width), kind),
            pltpu.VMEM((count, rows, width), kind),
            pltpu.VMEM((quarter, rows, width), kind),
            pltpu.VMEM((quarter, rows, width), kind),
            pltpu.VMEM((quarter, rows, width), kind),
            pltpu.VMEM((groups, width, 2, width), kind),
            pltpu.VMEM((groups, width, width), kind),
            pltpu.VMEM((groups, width, width), kind),
            pltpu.VMEM((groups, width, width), kind),
            dma((count,)),
            dma((count,)),
            dma((count,)),
            dma((count,)),
            dma((2, quarter)),
            dma((count // 2,)),
            dma((quarter + 1,)),
            dma((groups,)),
            dma((2, groups)),
            dma((3,)),
            pltpu.SemaphoreType.REGULAR,
        ],
        compiler_params=pltpu.CompilerParams(
            collective_id=0, has_side_effects=True, vmem_limit_bytes=48 * 1024 * 1024
        ),
    )(
        *[
            pltpu.with_memory_space_constraint(operand, pltpu.HBM)
            for operand in (orbital_irrep, slab_irrep, virtual_count, amplitudes, integrals)
        ]
    )


def solution(mesh):
    in_specs = (
        P(("parts", "row"), "col", None, None),
        P(("parts", "col"), None, None, None),
        P("parts"),
        P("parts"),
        P("parts"),
    )
    return jax.shard_map(
        functools.partial(per_device, count=mesh.shape["row"]),
        mesh=mesh,
        in_specs=in_specs,
        out_specs=P("parts", "col", "row", None),
        check_vma=False,
    )
```

```python
import functools

import jax
import jax.numpy as jnp
from jax import lax
from jax.experimental import pallas as pl
from jax.experimental.pallas import tpu as pltpu
from jax.sharding import PartitionSpec as P

MESH = pl.DeviceIdType.MESH


def partner_of(me, step, count, back=False):
    if count & (count - 1):
        return (me + (count - step if back else step)) % count
    place, bit = 0, 1
    while bit < count:
        place = place + (((me // bit) % 2 + (step // bit) % 2) % 2) * bit
        bit *= 2
    return place


def each(low, high, body):
    if high - low <= 16:
        for step in range(low, high):
            body(step)
    else:
        lax.fori_loop(low, high, lambda step, carry: (body(step), carry)[1], 0)


def kernel(
    count,
    label_hbm, slab_hbm, size_hbm, amp_ref, int_ref, out_ref,
    label_ref, slab_ref, size_ref, landed, shared, late_own, late_shared, staged, raw, own_tiles, sent_tiles, other_tiles,
    send_sem, land_sem, pass_sem, share_sem, late_sem, done_sem, own_sem, raw_sem, tile_sem, label_sem, ready_sem,
):
    me = lax.axis_index("row")
    col = lax.axis_index("col")
    sibling = 1 - col
    rows, width = landed.shape[1:]
    groups = own_tiles.shape[0]
    quarter = count // 4
    near, late = count // 2, count - quarter
    last = me // late
    odd = (me // quarter) % 2

    def target(step):
        return partner_of(me, step, count)

    def source(step):
        return partner_of(me, step, count, back=True)

    def block_of(there):
        return amp_ref.at[0, 0, pl.ds(pl.multiple_of(there * rows, rows), rows)]

    raw_copies = [
        pltpu.make_async_copy(
            int_ref.at[0, pl.ds(e * width, width)], raw.at[e], raw_sem.at[e]
        )
        for e in range(groups)
    ]
    label_copies = [
        pltpu.make_async_copy(origin, place, label_sem.at[number])
        for number, (origin, place) in enumerate(
            [(label_hbm, label_ref), (slab_hbm, slab_ref), (size_hbm, size_ref)]
        )
    ]

    def late_step(slot):
        return late + slot - quarter * odd

    own_copy = pltpu.make_async_copy(block_of(me), landed.at[me], own_sem.at[quarter])

    def late_copy(slot):
        return pltpu.make_async_copy(
            block_of(target(late_step(slot))), late_own.at[slot], own_sem.at[slot]
        )

    def late_share(slot):
        return pltpu.make_async_remote_copy(
            src_ref=block_of(target(late_step(slot))),
            dst_ref=late_shared.at[slot],
            send_sem=late_sem.at[0, slot],
            recv_sem=late_sem.at[1, slot],
            device_id={"col": sibling},
            device_id_type=MESH,
        )

    def spread_copy(step):
        there = target(step)
        return pltpu.make_async_remote_copy(
            src_ref=block_of(there),
            dst_ref=landed.at[me],
            send_sem=send_sem.at[step],
            recv_sem=land_sem.at[step],
            device_id={"row": there},
            device_id_type=MESH,
        )

    def share_copy(step):
        slot = source(step)
        return pltpu.make_async_remote_copy(
            src_ref=landed.at[slot],
            dst_ref=shared.at[slot],
            send_sem=pass_sem.at[step],
            recv_sem=share_sem.at[step],
            device_id={"col": sibling},
            device_id_type=MESH,
        )

    def done_copy(step, slot):
        return pltpu.make_async_remote_copy(
            src_ref=staged.at[slot],
            dst_ref=out_ref.at[me, 0],
            send_sem=send_sem.at[step],
            recv_sem=done_sem.at[step - near],
            device_id={"row": target(step)},
            device_id_type=MESH,
        )

    for copy in label_copies + raw_copies:
        copy.start()
    each(0, quarter, lambda slot: late_copy(slot).start())
    own_copy.start()

    barrier = pltpu.get_barrier_semaphore()

    def signal(semaphore, step):
        pl.semaphore_signal(
            semaphore, inc=1, device_id={"row": target(step)}, device_id_type=MESH
        )

    each(1, quarter, lambda step: signal(barrier, step))
    pl.semaphore_signal(barrier, inc=1, device_id={"col": sibling}, device_id_type=MESH)

    @pl.when(last == 0)
    def _():
        each(quarter, count, lambda step: signal(barrier, step))

    pl.semaphore_wait(barrier, count - quarter * (1 - last))

    @pl.when(last == 1)
    def _():
        each(quarter, count, lambda step: signal(ready_sem, step))

    def send_now(step):
        @pl.when(last + 1 > target(step) // late)
        def _():
            spread_copy(step).start()

    def send_when_ready(step):
        @pl.when(last < target(step) // late)
        def _():
            spread_copy(step).start()

    each(near, late, lambda step: spread_copy(step + quarter * odd).start())
    each(1, near, send_now)

    @pl.when(last == 0)
    def _():
        pl.semaphore_wait(ready_sem, quarter)

    each(1, near, send_when_ready)
    each(0, quarter, lambda slot: late_share(slot).start())
    for copy in label_copies:
        copy.wait()

    own_label = slab_ref[col]
    other_label = slab_ref[sibling]
    place = lax.broadcasted_iota(jnp.int32, (width, width), 0)
    column = lax.broadcasted_iota(jnp.int32, (width, width), 1)

    def keep(tile, e, j):
        outer = size_ref[e ^ own_label ^ slab_ref[2 + j]]
        return jnp.where((place < size_ref[e]) & (column < outer), tile, jnp.zeros((), tile.dtype))

    tile_copies = []
    for e in range(groups):
        raw_copies[e].wait()
        tile_pair = raw[e]
        first = tile_pair[:, 0, :]
        second = tile_pair[:, 1, :]
        mine = jnp.where(col == 0, first, second)
        other = jnp.where(col == 0, second, first)
        sent_tiles[e] = keep(other, e, sibling)
        copy = pltpu.make_async_remote_copy(
            src_ref=sent_tiles.at[e],
            dst_ref=other_tiles.at[e],
            send_sem=tile_sem.at[0, e],
            recv_sem=tile_sem.at[1, e],
            device_id={"col": sibling},
            device_id_type=MESH,
        )
        copy.start()
        tile_copies.append(copy)
        own_tiles[e] = keep(mine, e, col)
    for copy in tile_copies:
        copy.wait_recv()

    row_place = lax.broadcasted_iota(jnp.int32, (rows, width), 0)

    def product(mine, other, there, orbital):
        first_virtual = there * rows
        group = first_virtual // width
        label = group ^ label_ref[orbital]
        total = jnp.dot(
            mine, own_tiles[label ^ own_label], preferred_element_type=jnp.float32
        )
        total = total + jnp.dot(
            other, other_tiles[label ^ other_label], preferred_element_type=jnp.float32
        )
        real = row_place + first_virtual % width < size_ref[group]
        return jnp.where(real, total, 0.0).astype(out_ref.dtype)

    def depart(slot):
        late_copy(slot).wait()
        late_share(slot).wait_recv()
        step = late_step(slot)
        staged[slot] = product(late_own[slot], late_shared[slot], target(step), me)
        done_copy(step, slot).start()

    each(0, quarter, lambda slot: depart(quarter - 1 - slot))

    own_copy.wait()
    share_copy(0).start()

    def finish(step):
        share_copy(step).wait_recv()
        there = source(step)
        out_ref[there, 0] = product(landed[there], shared[there], me, there)

    def arrive(step):
        spread_copy(step).wait_recv()
        share_copy(step).start()

    def arrive_then_finish(step):
        arrive(step)
        finish(step - 1)

    each(1, near, arrive_then_finish)

    @pl.when(odd == 0)
    def _():
        each(near, count, arrive_then_finish)
        finish(count - 1)

    @pl.when(odd == 1)
    def _():
        finish(near - 1)

    for copy in tile_copies:
        copy.wait_send()
    each(1, near, lambda step: spread_copy(step).wait_send())
    each(near, late, lambda step: spread_copy(step + quarter * odd).wait_send())
    each(0, quarter, lambda slot: done_copy(late_step(slot), slot).wait_send())
    each(0, quarter, lambda slot: late_share(slot).wait_send())
    each(0, near, lambda step: share_copy(step).wait_send())

    @pl.when(odd == 0)
    def _():
        each(near, count, lambda step: share_copy(step).wait_send())

    @pl.when(odd == 1)
    def _():
        each(near, count, lambda step: done_copy(step, 0).wait_recv())


def per_device(amplitudes, integrals, orbital_irrep, slab_irrep, virtual_count, count):
    virtual_total, width = amplitudes.shape[2:]
    groups = virtual_count.shape[0]
    rows = virtual_total // count
    quarter = count // 4
    kind = amplitudes.dtype
    dma = pltpu.SemaphoreType.DMA
    return pl.pallas_call(
        functools.partial(kernel, count),
        out_shape=pltpu.VMEM((count, 1, rows, width), kind),
        in_specs=[pl.BlockSpec(memory_space=pltpu.HBM)] * 5,
        out_specs=pl.BlockSpec(memory_space=pltpu.VMEM),
        scratch_shapes=[
            pltpu.SMEM(orbital_irrep.shape, jnp.int32),
            pltpu.SMEM(slab_irrep.shape, jnp.int32),
            pltpu.SMEM(virtual_count.shape, jnp.int32),
            pltpu.VMEM((count, rows, width), kind),
            pltpu.VMEM((count, rows, width), kind),
            pltpu.VMEM((quarter, rows, width), kind),
            pltpu.VMEM((quarter, rows, width), kind),
            pltpu.VMEM((quarter, rows, width), kind),
            pltpu.VMEM((groups, width, 2, width), kind),
            pltpu.VMEM((groups, width, width), kind),
            pltpu.VMEM((groups, width, width), kind),
            pltpu.VMEM((groups, width, width), kind),
            dma((count,)),
            dma((count,)),
            dma((count,)),
            dma((count,)),
            dma((2, quarter)),
            dma((count // 2,)),
            dma((quarter + 1,)),
            dma((groups,)),
            dma((2, groups)),
            dma((3,)),
            pltpu.SemaphoreType.REGULAR,
        ],
        compiler_params=pltpu.CompilerParams(
            collective_id=0, has_side_effects=True, vmem_limit_bytes=48 * 1024 * 1024
        ),
    )(
        *[
            pltpu.with_memory_space_constraint(operand, pltpu.HBM)
            for operand in (orbital_irrep, slab_irrep, virtual_count, amplitudes, integrals)
        ]
    )


def solution(mesh):
    in_specs = (
        P(("parts", "row"), "col", None, None),
        P(("parts", "col"), None, None, None),
        P("parts"),
        P("parts"),
        P("parts"),
    )
    return jax.shard_map(
        functools.partial(per_device, count=mesh.shape["row"]),
        mesh=mesh,
        in_specs=in_specs,
        out_specs=P("parts", "col", "row", None),
        check_vma=False,
    )
```
